32 devices in a mesh: groups: 2 (over y), row: 4 (over x, core), col: 4 (over z).
Axes of the slice: x: 2, y: 2, z: 4, core: 2. Of those that a mesh axis runs over, the one named last changes fastest.
Arguments:
- queries: bfloat16 [2048, 384], P(('groups', 'row', 'col')), parts along dimension 0, may hold values from -90 to 90
- keys: bfloat16 [2048, 384], P(('groups', 'col', 'row')), parts along dimension 0, may hold values from -15 to 15
- values: bfloat16 [2048, 384], P(('groups', 'col', 'row')), parts along dimension 0, may hold values from -6 to 6
- block_mask: int32 [16, 8], P(('groups', 'row'), 'col'), parts along dimension 0, may hold values from 0 to 1, as said below
- out_weight: bfloat16 [384, 2560], P(None, ('row', 'col')), may hold values from -0.3125 to 0.3125
- residual: bfloat16 [2048, 2560], P(('groups', 'row', 'col')), parts along dimension 0, may hold values from -1.5 to 1.5
Outputs:
- block_out: bfloat16 [2048, 2560], P(('groups', 'row', 'col')), parts along dimension 0
The draws below stay inside these ranges and needn't reach their ends.
There are 2 independent parts, one for each index of `groups`. The reference program is written for one: setup_inputs(seed, part) draws one part's arguments, and reference() takes and returns one part's arrays. A program takes and returns all parts, laid end to end along the dimension named above; an argument that names none is the same for every part. Nothing has to cross between parts.
Inputs may be any that keep to these rules, and one draw needn't show every extreme that they name: Entries are 0 or 1; block_mask[b, b] = 1 for every b. Each query block keeps between 1 and 2 key blocks in each key tile of 2 blocks, and in every pair of a query tile of 2 blocks and a key tile some query block keeps exactly 2.
All inputs are finite; a program needn't handle non-finite values.
Results may differ from the reference program's by a relative error of at most 0.0035.
Values may be sent and summed in bfloat16 or wider, within the bound.
No kernel may reach another device: no remote copies, remote signals or barrier semaphores. Data moves between devices by JAX's collectives and lax.ppermute only.
A program may use at most 64 MiB of HBM per device.

```python
import math
import jax
import jax.numpy as jnp
from jax import lax

HD = 128
HEADS = 3
DOUT = 2560
BLK = 128
TOKENS = 1024
NB = 8
QBT = 2
KBT = 2
KEEP_MOST = 2


def paired_fields(key):
    key_query = jax.random.fold_in(key, 11)
    key_key = jax.random.fold_in(key, 12)
    query_field = jnp.clip(jax.random.normal(key_query, (TOKENS, HEADS, HD), jnp.float32), -6.0, 6.0)
    key_field = jnp.clip(2.5 * jax.random.normal(key_key, (TOKENS, HEADS, HD), jnp.float32), -15.0, 15.0)
    return (query_field.reshape(TOKENS, HEADS * HD), key_field.reshape(TOKENS, HEADS * HD))


def draw_queries(key, part):
    query_field, key_field = paired_fields(key)
    return query_field.astype(jnp.bfloat16)


def draw_keys(key, part):
    query_field, key_field = paired_fields(key)
    return key_field.astype(jnp.bfloat16)


def draw_block_mask(key, part):
    tiles = NB // KBT
    first, second, third = jax.random.split(jax.random.fold_in(key, 21), 3)
    within = jnp.arange(KBT, dtype=jnp.int32)
    noise = jax.random.randint(first, (NB, tiles, KBT), 0, 2 ** 20) * KBT + within[None, None, :]
    column = jnp.arange(tiles, dtype=jnp.int32)[None, :, None] * KBT + within[None, None, :]
    row_index = jnp.arange(NB, dtype=jnp.int32)[:, None, None]
    noise = jnp.where(column == row_index, -1, noise)
    ranking = jnp.argsort(jnp.argsort(noise, axis=-1, stable=True), axis=-1, stable=True)
    counts = jax.random.randint(second, (NB, tiles), 1, KEEP_MOST + 1)
    chosen_row = jax.random.randint(third, (NB // QBT, tiles), 0, QBT)
    position = (jnp.arange(NB, dtype=jnp.int32) % QBT)[:, None]
    forced = jnp.repeat(chosen_row, QBT, axis=0)
    counts = jnp.where(position == forced, KEEP_MOST, counts)
    kept = ranking < counts[:, :, None]
    return kept.astype(jnp.int32).reshape(NB, NB)


def steps_of(own_key, extent, shards, smallest, largest):
    loudness, own = 1.0, jax.random.fold_in(own_key, 6)
    for dim, parts in shards:
        draws = jnp.exp(jax.random.uniform(jax.random.fold_in(own, dim), (parts,), jnp.float32, smallest / len(shards), largest / len(shards)))
        loudness = loudness * jnp.repeat(draws, extent[dim] // parts).reshape([-1 if axis == dim else 1 for axis in range(len(extent))])
    return loudness


def normal_values(own_key, extent, spread, bound, cuts=(), kind=jnp.bfloat16):
    loudness = steps_of(own_key, extent, cuts, -0.22, 0.18) if cuts else 1.0
    values = jax.random.normal(own_key, extent, jnp.float32) * spread * loudness
    return jnp.minimum(jnp.maximum(values, -bound), bound).astype(kind)


def setup_inputs(seed: int = 0, part: int = 0) -> dict:
    key_of = jax.random.split(jax.random.key(seed), 7)
    part_splits = jax.random.split(jax.random.fold_in(key_of[6], part), 7)
    return {
        "queries": draw_queries(jax.random.fold_in(jax.random.fold_in(key_of[6], part), 71), part),
        "keys": draw_keys(jax.random.fold_in(jax.random.fold_in(key_of[6], part), 71), part),
        "values": normal_values(part_splits[2], (TOKENS, HEADS * HD), 1.0, 6.0, ((0, 16),)),
        "block_mask": draw_block_mask(jax.random.fold_in(jax.random.fold_in(key_of[6], part), 71), part),
        "out_weight": normal_values(key_of[4], (HEADS * HD, DOUT), (HEADS * HD) ** -0.5, 0.3125, ((1, 16),)),
        "residual": normal_values(part_splits[5], (TOKENS, DOUT), 0.25, 1.5, ((0, 16),)),
    }


def reference(queries, keys, values, block_mask, out_weight, residual):
    score_scale = 1.0 / math.sqrt(HD)
    query_heads = queries.reshape(TOKENS, HEADS, HD)
    key_blocks = keys.reshape(NB, BLK, HEADS, HD)
    value_blocks = values.reshape(NB, BLK, HEADS, HD)
    tiles = NB // KBT
    mask_tiles = block_mask.reshape(NB, tiles, KBT)
    within = jnp.arange(KBT, dtype=jnp.int32)
    tile_start = (jnp.arange(tiles, dtype=jnp.int32) * KBT)[:, None]

    def one_block(index):
        query_rows = lax.dynamic_slice_in_dim(query_heads, (index * BLK).astype(jnp.int32), BLK, 0).astype(jnp.float32)
        mask_row = mask_tiles[index]
        priority = mask_row * (2 * KBT) + (KBT - within)[None, :]
        top_values, chosen = lax.top_k(priority, KEEP_MOST)
        chosen = chosen.astype(jnp.int32)
        usable = jnp.take_along_axis(mask_row, chosen, axis=1) > 0
        picked = (tile_start + chosen).astype(jnp.int32)
        near_keys = key_blocks[picked].astype(jnp.float32)
        near_values = value_blocks[picked].astype(jnp.float32)
        scores = jnp.einsum('qhd,tkbhd->qhtkb', query_rows, near_keys) * score_scale
        scores = jnp.where(usable[None, None, :, :, None], scores, -jnp.inf)
        tile_max = lax.optimization_barrier(jnp.max(scores, axis=(3, 4)))
        weights = jnp.exp(scores - tile_max[:, :, :, None, None])
        tile_total = lax.optimization_barrier(jnp.sum(weights, axis=(3, 4)))
        rounded = lax.optimization_barrier(weights.astype(jnp.bfloat16))
        tile_sum = jnp.einsum('qhtkb,tkbhd->qhtd', rounded.astype(jnp.float32), near_values)
        row_max = lax.optimization_barrier(jnp.max(tile_max, axis=2))
        factor = jnp.exp(tile_max - row_max[:, :, None])
        numer = lax.optimization_barrier(jnp.sum(tile_sum * factor[:, :, :, None], axis=2))
        denom = lax.optimization_barrier(jnp.sum(tile_total * factor, axis=2))
        return (numer / denom[:, :, None]).astype(jnp.bfloat16)
    attended = lax.map(one_block, jnp.arange(NB, dtype=jnp.int32)).reshape(TOKENS, HEADS * HD)
    projected = jnp.dot(attended, out_weight, preferred_element_type=jnp.float32)
    return (projected + residual.astype(jnp.float32)).astype(jnp.bfloat16)
```

```python
import functools
import math

import jax
import jax.numpy as jnp
from jax import lax
from jax.experimental import pallas as pl
from jax.experimental.pallas import tpu as pltpu
from jax.sharding import PartitionSpec as P

HD = 128
BLK = 128
LANES = 128
PARTS = 3


def swap(x, axis, mask):
    return lax.ppermute(x, axis, [(i, i ^ mask) for i in range(lax.axis_size(axis))])


def split3(x):
    high = x.astype(jnp.bfloat16).astype(jnp.float32)
    rest = x - high
    middle = rest.astype(jnp.bfloat16).astype(jnp.float32)
    return (high, middle, rest - middle)


def attend_kernel(q_masks, k_masks, where_ref, mask_ref, *refs):
    nq, nk = len(q_masks), len(k_masks)
    q_refs, k_refs, v_refs = refs[:nq], refs[nq : nq + nk], refs[nq + nk : nq + 2 * nk]
    out_refs = refs[nq + 2 * nk : 2 * nq + 2 * nk]
    rows, width = q_refs[0].shape
    heads = width // HD
    scale = 1.0 / math.sqrt(HD)
    my_row, my_col = where_ref[0], where_ref[1]
    keys = nk * rows
    piece_of_lane = lax.broadcasted_iota(jnp.int32, (1, keys), 1) // rows
    group = min(nq, 4)
    lane = lax.broadcasted_iota(jnp.int32, (group * rows, LANES), 1)
    for first in range(0, nq, group):
        chosen = range(first, first + group)
        lines = []
        for i in chosen:
            q_block = ((my_col ^ q_masks[i]) * rows) // BLK
            line = jnp.zeros((1, keys), jnp.float32)
            for j in range(nk):
                k_block = ((my_row ^ k_masks[j]) * rows) // BLK
                hidden = jnp.where(mask_ref[q_block, k_block] == 1, 0.0, -jnp.inf)
                line = jnp.where(piece_of_lane == j, hidden, line)
            lines.append(jnp.broadcast_to(line, (rows, keys)))
        bias = jnp.concatenate(lines, axis=0)
        stats = jnp.zeros((group * rows, LANES), jnp.float32)
        for h in range(heads):
            columns = slice(h * HD, (h + 1) * HD)
            q = jnp.concatenate([q_refs[i][:, columns] for i in chosen], axis=0)
            k = jnp.concatenate([r[:, columns] for r in k_refs], axis=0)
            v = jnp.concatenate([r[:, columns] for r in v_refs], axis=0)
            scores = lax.dot_general(
                q, k, (((1,), (1,)), ((), ())), preferred_element_type=jnp.float32
            )
            scores = scores * scale + bias
            top = jnp.max(scores, axis=1, keepdims=True)
            weights = jnp.exp(scores - top)
            total = jnp.sum(weights, axis=1, keepdims=True)
            summed = jnp.dot(weights.astype(jnp.bfloat16), v, preferred_element_type=jnp.float32)
            mean = (summed / total).astype(jnp.bfloat16)
            for n, i in enumerate(chosen):
                out_refs[i][:, columns] = mean[n * rows : (n + 1) * rows]
            for n, piece in enumerate(split3(top) + split3(total)):
                stats = jnp.where(lane == h * 2 * PARTS + n, piece, stats)
        stats = stats.astype(jnp.bfloat16)
        for n, i in enumerate(chosen):
            out_refs[i][:, width:] = stats[n * rows : (n + 1) * rows]


def attend(where, mask, q_parts, k_parts, v_parts):
    q_masks, k_masks = tuple(q_parts), tuple(k_parts)
    rows, width = q_parts[0].shape
    smem = pl.BlockSpec(memory_space=pltpu.SMEM)
    vmem = pl.BlockSpec(memory_space=pltpu.VMEM)
    arrays = [*q_parts.values(), *k_parts.values(), *v_parts.values()]
    outs = pl.pallas_call(
        functools.partial(attend_kernel, q_masks, k_masks),
        out_shape=[jax.ShapeDtypeStruct((rows, width + LANES), jnp.bfloat16)] * len(q_masks),
        in_specs=[smem, smem] + [vmem] * len(arrays),
        out_specs=[vmem] * len(q_masks),
        compiler_params=pltpu.CompilerParams(vmem_limit_bytes=24 * 2**20),
    )(where, mask, *arrays)
    return dict(zip(q_masks, outs))


def project_kernel(n_parts, w_ids, n_col, where_ref, *refs):
    part_refs = refs[:n_parts]
    w_refs = refs[n_parts : n_parts + len(w_ids)]
    residual_ref, out_ref, whole_ref = refs[n_parts + len(w_ids) :]
    rows, width = out_ref.shape[0], whole_ref.shape[1]
    heads = width // HD
    my_row, my_col = where_ref[0], where_ref[1]
    for (a, b), ref in zip(w_ids, w_refs):
        depth = ref.shape[0]
        place = ((my_row ^ a) * n_col + (my_col ^ b)) * depth
        whole_ref[pl.ds(pl.multiple_of(place, 16), depth), :] = ref[...]
    stats = [ref[:, width:].astype(jnp.float32) for ref in part_refs]
    attended = []
    for h in range(heads):
        columns = slice(h * HD, (h + 1) * HD)
        first = h * 2 * PARTS
        tops = [s[:, first : first + 1] + s[:, first + 1 : first + 2] + s[:, first + 2 : first + 3] for s in stats]
        first += PARTS
        totals = [s[:, first : first + 1] + s[:, first + 1 : first + 2] + s[:, first + 2 : first + 3] for s in stats]
        top = functools.reduce(jnp.maximum, tops)
        shares = [jnp.exp(t - top) * n for t, n in zip(tops, totals)]
        denom = functools.reduce(jnp.add, shares)
        numer = functools.reduce(
            jnp.add, [ref[:, columns].astype(jnp.float32) * s for ref, s in zip(part_refs, shares)]
        )
        attended.append((numer / denom).astype(jnp.bfloat16))
    attended = jnp.concatenate(attended, axis=1)
    features = out_ref.shape[1]
    step = features // 4 if features % (4 * LANES) == 0 else features
    for at in range(0, features, step):
        here = slice(at, at + step)
        product = lax.dot_general(
            attended, whole_ref[here, :], (((1,), (1,)), ((), ())), preferred_element_type=jnp.float32
        )
        out_ref[:, here] = (product + residual_ref[:, here].astype(jnp.float32)).astype(out_ref.dtype)


def project(where, parts, w_parts, residual, n_col):
    w_ids = tuple(w_parts)
    rows, features = residual.shape
    width = w_parts[w_ids[0]].shape[1]
    smem = pl.BlockSpec(memory_space=pltpu.SMEM)
    vmem = pl.BlockSpec(memory_space=pltpu.VMEM)
    arrays = [*parts.values(), *w_parts.values(), residual]
    return pl.pallas_call(
        functools.partial(project_kernel, len(parts), w_ids, n_col),
        out_shape=jax.ShapeDtypeStruct((rows, features), residual.dtype),
        in_specs=[smem] + [vmem] * len(arrays),
        out_specs=vmem,
        scratch_shapes=[pltpu.VMEM((features, width), jnp.bfloat16)],
        compiler_params=pltpu.CompilerParams(vmem_limit_bytes=24 * 2**20),
    )(where, *arrays)


def local(queries, keys, values, block_mask, out_weight, residual):
    n_row, n_col = lax.axis_size("row"), lax.axis_size("col")
    far = range(n_col - 1, 0, -1)
    chips = range(2, n_row, 2)
    where = jnp.stack([lax.axis_index("row"), lax.axis_index("col")]).astype(jnp.int32)

    q_parts = {0: queries}
    for m in far:
        q_parts[m] = swap(queries, "col", m)
    k_parts, v_parts = {0: keys}, {0: values}
    for m in chips:
        k_parts[m] = swap(keys, "row", m)
        v_parts[m] = swap(values, "row", m)
    for m in (0, *chips):
        k_parts[m | 1] = swap(k_parts[m], "row", 1)
        v_parts[m | 1] = swap(v_parts[m], "row", 1)

    depth = out_weight.shape[1]
    if depth % 16 == 0:
        w_parts = {(0, 0): out_weight.T}
        for m in far:
            w_parts[0, m] = swap(w_parts[0, 0], "col", m)
        for b in (0, *far):
            for a in chips:
                w_parts[a, b] = swap(w_parts[0, b], "row", a)
        for a, b in list(w_parts):
            w_parts[a | 1, b] = swap(w_parts[a, b], "row", 1)
    else:
        gathered = lax.all_gather(out_weight, ("row", "col"), axis=1, tiled=True)
        w_parts = None

    partial = attend(where, block_mask, q_parts, k_parts, v_parts)
    parts = {0: partial[0]}
    for m in far:
        parts[m] = swap(partial[m], "col", m)
    if w_parts is None:
        zero = jnp.zeros((2,), jnp.int32)
        return project(zero, parts, {(0, 0): gathered.T}, residual, 1)
    return project(where, parts, w_parts, residual, n_col)


def solution(mesh):
    placed = (
        P(("groups", "row", "col"), None),
        P(("groups", "col", "row"), None),
        P(("groups", "col", "row"), None),
        P(("groups", "row"), "col"),
        P(None, ("row", "col")),
        P(("groups", "row", "col"), None),
    )
    return jax.shard_map(
        local,
        mesh=mesh,
        in_specs=placed,
        out_specs=P(("groups", "row", "col"), None),
        check_vma=False,
    )
```

```python
import functools
import math

import jax
import jax.numpy as jnp
from jax import lax
from jax.experimental import pallas as pl
from jax.experimental.pallas import tpu as pltpu
from jax.sharding import PartitionSpec as P

HD = 128
BLK = 128
LANES = 128
PARTS = 3
SPAN = 8192.0


def swap(x, axis, mask):
    return lax.ppermute(x, axis, [(i, i ^ mask) for i in range(lax.axis_size(axis))])


def after(x, *others):
    return lax.optimization_barrier((x, *others))[0]


def split3(x):
    high = x.astype(jnp.bfloat16).astype(jnp.float32)
    rest = x - high
    middle = rest.astype(jnp.bfloat16).astype(jnp.float32)
    return (high, middle, rest - middle)


def attend_kernel(q_masks, k_masks, top, mask_shape, place_ref, *refs):
    nq, nk = len(q_masks), len(k_masks)
    q_refs, kv_refs, out_refs = refs[:nq], refs[nq : nq + nk], refs[nq + nk :]
    rows, width = q_refs[0].shape
    heads = width // HD
    scale = 1.0 / math.sqrt(HD)
    my_row, my_col = place_ref[0], place_ref[1]
    keys = nk * rows
    piece_of_lane = lax.broadcasted_iota(jnp.int32, (1, keys), 1) // rows
    group = min(nq, 4)
    lane = lax.broadcasted_iota(jnp.int32, (group * rows, LANES), 1)
    for first in range(0, nq, group):
        chosen = range(first, first + group)
        lines = []
        for i in chosen:
            q_block = ((my_col ^ q_masks[i]) * rows) // BLK
            line = jnp.zeros((1, keys), jnp.float32)
            for j, (a, b) in enumerate(k_masks):
                k_block = ((my_row ^ a) * rows) // BLK
                at = 2 + q_block * mask_shape[1] + k_block
                if b:
                    at += mask_shape[0] * mask_shape[1]
                hidden = jnp.where(place_ref[at] == 1, 0.0, -jnp.inf)
                line = jnp.where(piece_of_lane == j, hidden, line)
            lines.append(jnp.broadcast_to(line, (rows, keys)))
        bias = jnp.concatenate(lines, axis=0)
        stats = jnp.zeros((group * rows, LANES), jnp.float32)
        for h in range(heads):
            columns = slice(h * HD, (h + 1) * HD)
            q = jnp.concatenate([q_refs[i][:, columns] for i in chosen], axis=0)
            k = jnp.concatenate([r[:rows, columns] for r in kv_refs], axis=0)
            v = jnp.concatenate([r[rows : 2 * rows, columns] for r in kv_refs], axis=0)
            scores = lax.dot_general(
                q, k, (((1,), (1,)), ((), ())), preferred_element_type=jnp.float32
            )
            scores = scores * scale + bias
            top_score = jnp.max(scores, axis=1, keepdims=True)
            weights = jnp.exp(scores - top_score)
            total = jnp.sum(weights, axis=1, keepdims=True)
            summed = jnp.dot(weights.astype(jnp.bfloat16), v, preferred_element_type=jnp.float32)
            mean = summed * (SPAN / total)
            for n, i in enumerate(chosen):
                out_refs[i][:, columns] = mean[n * rows : (n + 1) * rows]
            for n, piece in enumerate(split3(top_score) + split3(total)):
                stats = jnp.where(lane == h * 2 * PARTS + n, piece, stats)
        for n, i in enumerate(chosen):
            out_refs[i][:, width:] = stats[n * rows : (n + 1) * rows]


def attend(place, mask_shape, top, q_parts, kv_parts):
    q_masks, k_masks = tuple(q_parts), tuple(kv_parts)
    rows, width = q_parts[0].shape
    smem = pl.BlockSpec(memory_space=pltpu.SMEM)
    vmem = pl.BlockSpec(memory_space=pltpu.VMEM)
    arrays = [*q_parts.values(), *kv_parts.values()]
    outs = pl.pallas_call(
        functools.partial(attend_kernel, q_masks, k_masks, top, mask_shape),
        out_shape=[jax.ShapeDtypeStruct((rows, width + LANES), jnp.float32)] * len(q_masks),
        in_specs=[smem] + [vmem] * len(arrays),
        out_specs=[vmem] * len(q_masks),
        compiler_params=pltpu.CompilerParams(vmem_limit_bytes=24 * 2**20),
    )(place, *arrays)
    return dict(zip(q_masks, outs))


def project_kernel(n_parts, w_ids, n_col, depth, where_ref, *refs):
    part_refs = refs[:n_parts]
    w_refs = refs[n_parts : n_parts + len(w_ids)]
    residual_ref, out_ref, whole_ref = refs[n_parts + len(w_ids) :]
    rows, width = out_ref.shape[0], whole_ref.shape[1]
    my_row, my_col = where_ref[0], where_ref[1]
    for ids, ref in zip(w_ids, w_refs):
        first = ref.shape[0] - len(ids) * depth
        for n, (a, b) in enumerate(ids):
            place = ((my_row ^ a) * n_col + (my_col ^ b)) * depth
            piece = ref[first + n * depth : first + (n + 1) * depth, :]
            whole_ref[pl.ds(pl.multiple_of(place, 16), depth), :] = piece
    source = lax.broadcasted_iota(jnp.int32, (LANES, 2 * width), 0) // PARTS
    target = lax.broadcasted_iota(jnp.int32, (LANES, 2 * width), 1)
    target = target % width // HD * 2 + target // width
    spread = (source == target).astype(jnp.bfloat16)
    tops, totals = [], []
    for ref in part_refs:
        stats = jnp.dot(ref[:, width:].astype(jnp.bfloat16), spread, preferred_element_type=jnp.float32)
        tops.append(stats[:, :width])
        totals.append(stats[:, width:])
    top = functools.reduce(jnp.maximum, tops)
    shares = [jnp.exp(t - top) * n for t, n in zip(tops, totals)]
    denom = functools.reduce(jnp.add, shares)
    numer = functools.reduce(jnp.add, [ref[:, :width] * s for ref, s in zip(part_refs, shares)])
    attended = (numer / (denom * SPAN)).astype(jnp.bfloat16)
    features = out_ref.shape[1]
    step = features // 4 if features % (4 * LANES) == 0 else features
    for at in range(0, features, step):
        here = slice(at, at + step)
        product = lax.dot_general(
            attended, whole_ref[here, :], (((1,), (1,)), ((), ())), preferred_element_type=jnp.float32
        )
        out_ref[:, here] = (product + residual_ref[:, here].astype(jnp.float32)).astype(out_ref.dtype)


def project(where, parts, w_parts, residual, n_col, depth):
    w_ids = [ids for _, ids in w_parts]
    rows, features = residual.shape
    width = w_parts[0][0].shape[1]
    smem = pl.BlockSpec(memory_space=pltpu.SMEM)
    vmem = pl.BlockSpec(memory_space=pltpu.VMEM)
    arrays = [*parts.values(), *(x for x, _ in w_parts), residual]
    return pl.pallas_call(
        functools.partial(project_kernel, len(parts), w_ids, n_col, depth),
        out_shape=jax.ShapeDtypeStruct((rows, features), residual.dtype),
        in_specs=[smem] + [vmem] * len(arrays),
        out_specs=vmem,
        scratch_shapes=[pltpu.VMEM((features, width), jnp.bfloat16)],
        compiler_params=pltpu.CompilerParams(vmem_limit_bytes=24 * 2**20),
    )(where, *arrays)


def local(queries, keys, values, block_mask, out_weight, residual):
    n_row, n_col = lax.axis_size("row"), lax.axis_size("col")
    top = n_col // 2
    near = range(1, max(top, 1))
    chips = range(2, n_row, 2)
    rows, depth = queries.shape[0], out_weight.shape[1]
    ride = depth % 16 == 0
    where = jnp.stack([lax.axis_index("row"), lax.axis_index("col")]).astype(jnp.int32)
    weight = out_weight.T

    pack = jnp.concatenate([keys, values, weight] if ride else [keys, values])
    kv_parts = {(0, 0): pack}
    if top:
        far_k, far_v = swap(keys, "col", top), swap(values, "col", top)
        far_mask = swap(block_mask, "col", top)
    q_parts = {0: queries}
    for m in near:
        q_parts[m] = swap(queries, "col", m)
    for a in chips:
        kv_parts[a, 0] = swap(pack, "row", a)
    for a in (0, *chips):
        kv_parts[a | 1, 0] = swap(kv_parts[a, 0], "row", 1)
    gate = tuple(q_parts[m] for m in near) + ((far_mask,) if top else ())
    masks = [where, block_mask.reshape(-1)]
    if top:
        kv_parts[0, top] = jnp.concatenate([after(far_k, *gate), far_v])
        for a in chips:
            kv_parts[a, top] = swap(kv_parts[0, top], "row", a)
        for a in (0, *chips):
            kv_parts[a | 1, top] = swap(kv_parts[a, top], "row", 1)
        masks.append(far_mask.reshape(-1))
    place = jnp.concatenate(masks)
    partial = attend(place, block_mask.shape, top, q_parts, kv_parts)
    parts = {0: partial[0]}
    for m in near:
        parts[m] = swap(partial[m].astype(jnp.float16), "col", m).astype(jnp.float32)

    if not ride:
        gathered = lax.all_gather(weight, ("row", "col"), axis=0, tiled=True)
        return project(jnp.zeros_like(where), parts, [(gathered, [(0, 0)])], residual, 1, gathered.shape[0])
    w_parts = [(kv_parts[a, 0], [(a, 0)]) for a in range(n_row)]
    received = tuple(parts[m] for m in near)
    mine = [(weight, 0)]
    bit = top
    while bit:
        mine += [(swap(after(x, kv_parts[1, top]) if m else x, "col", bit), m | bit) for x, m in mine]
        bit //= 2
    for n, batch in enumerate((mine[1:-1], mine[-1:])):
        if not batch:
            continue
        batch = [(after(x, kv_parts[1, top]), m) for x, m in batch]
        block = jnp.concatenate([x for x, _ in batch]) if len(batch) > 1 else batch[0][0]
        cols = [m for _, m in batch]
        if n:
            block = after(block, partial[0])
        held = {0: block}
        for a in chips:
            held[a] = swap(block, "row", a)
        for a in (0, *chips):
            held[a | 1] = swap(after(held[a], *received), "row", 1)
        w_parts += [(x, [(a, m) for m in cols]) for a, x in held.items()]
    return project(where, parts, w_parts, residual, n_col, depth)


def solution(mesh):
    placed = (
        P(("groups", "row", "col"), None),
        P(("groups", "col", "row"), None),
        P(("groups", "col", "row"), None),
        P(("groups", "row"), "col"),
        P(None, ("row", "col")),
        P(("groups", "row", "col"), None),
    )
    return jax.shard_map(
        local,
        mesh=mesh,
        in_specs=placed,
        out_specs=P(("groups", "row", "col"), None),
        check_vma=False,
    )
```

```python
import functools
import math

import jax
import jax.numpy as jnp
from jax import lax
from jax.experimental import pallas as pl
from jax.experimental.pallas import tpu as pltpu
from jax.sharding import PartitionSpec as P

HD = 128
BLK = 128
LANES = 128
PARTS = 3
SPAN = 8192.0


def swap(x, axis, mask):
    return lax.ppermute(x, axis, [(i, i ^ mask) for i in range(lax.axis_size(axis))])


def after(x, *others):
    return lax.optimization_barrier((x, *others))[0]


def split3(x):
    high = x.astype(jnp.bfloat16).astype(jnp.float32)
    rest = x - high
    middle = rest.astype(jnp.bfloat16).astype(jnp.float32)
    return (high, middle, rest - middle)


def attend_kernel(q_masks, k_masks, per_tile, mask_shape, place_ref, *refs):
    nq, nk = len(q_masks), len(k_masks)
    q_refs, kv_refs, out_ref = refs[:nq], refs[nq : nq + nk], refs[-1]
    rows, width = q_refs[0].shape
    heads = width // HD
    scale = 1.0 / math.sqrt(HD)
    my_row, my_col = place_ref[0], place_ref[1]
    keys = nk * rows
    piece_of_lane = lax.broadcasted_iota(jnp.int32, (1, keys), 1) // rows
    group = min(nq, 4)
    lane = lax.broadcasted_iota(jnp.int32, (group * rows, LANES), 1)
    for first in range(0, nq, group):
        chosen = range(first, first + group)
        lines = []
        for i in chosen:
            q_block = ((my_col ^ q_masks[i]) * rows) // BLK
            line = jnp.zeros((1, keys), jnp.float32)
            for j, (a, b) in enumerate(k_masks):
                k_block = ((my_row ^ a) * rows) // BLK
                at = 2 + q_block * mask_shape[1] + k_block
                if b:
                    at += mask_shape[0] * mask_shape[1]
                hidden = jnp.where(place_ref[at] == 1, 0.0, -jnp.inf)
                line = jnp.where(piece_of_lane == j, hidden, line)
            lines.append(jnp.broadcast_to(line, (rows, keys)))
        bias = jnp.concatenate(lines, axis=0)
        stats = jnp.zeros((group * rows, LANES), jnp.float32)
        here = slice(first * rows, (first + group) * rows)
        for h in range(heads):
            columns = slice(h * HD, (h + 1) * HD)
            q = jnp.concatenate([q_refs[i][:rows, columns] for i in chosen], axis=0)
            tops, totals, sums = [], [], []
            for tile in range(0, nk, per_tile):
                refs_here = kv_refs[tile : tile + per_tile]
                k = jnp.concatenate([r[:rows, columns] for r in refs_here], axis=0)
                v = jnp.concatenate([r[rows : 2 * rows, columns] for r in refs_here], axis=0)
                scores = lax.dot_general(
                    q, k, (((1,), (1,)), ((), ())), preferred_element_type=jnp.float32
                )
                scores = scores * scale + bias[:, tile * rows : (tile + per_tile) * rows]
                tops.append(jnp.max(scores, axis=1, keepdims=True))
                weights = jnp.exp(scores - tops[-1])
                totals.append(jnp.sum(weights, axis=1, keepdims=True))
                sums.append(jnp.dot(weights.astype(jnp.bfloat16), v, preferred_element_type=jnp.float32))
            top_score = functools.reduce(jnp.maximum, tops)
            factors = [jnp.exp(t - top_score) for t in tops]
            total = functools.reduce(jnp.add, [f * t for f, t in zip(factors, totals)])
            summed = functools.reduce(jnp.add, [f * t for f, t in zip(factors, sums)])
            out_ref[here, columns] = summed * (SPAN / total)
            for n, piece in enumerate(split3(top_score) + split3(total)):
                stats = jnp.where(lane == h * 2 * PARTS + n, piece, stats)
        out_ref[here, width:] = stats


def attend(place, mask_shape, per_tile, q_parts, kv_parts):
    q_masks, k_masks = tuple(q_parts), tuple(kv_parts)
    rows, width = q_parts[0].shape
    smem = pl.BlockSpec(memory_space=pltpu.SMEM)
    vmem = pl.BlockSpec(memory_space=pltpu.VMEM)
    arrays = [*q_parts.values(), *kv_parts.values()]
    return pl.pallas_call(
        functools.partial(attend_kernel, q_masks, k_masks, per_tile, mask_shape),
        out_shape=jax.ShapeDtypeStruct((len(q_masks) * rows, width + LANES), jnp.float32),
        in_specs=[smem] + [vmem] * len(arrays),
        out_specs=vmem,
        compiler_params=pltpu.CompilerParams(vmem_limit_bytes=24 * 2**20),
    )(place, *arrays)


def merge(parts):
    width = parts[0].shape[1] - LANES
    source = lax.broadcasted_iota(jnp.int32, (LANES, 2 * width), 0) // PARTS
    target = lax.broadcasted_iota(jnp.int32, (LANES, 2 * width), 1)
    target = target % width // HD * 2 + target // width
    spread = (source == target).astype(jnp.bfloat16)
    tops, totals = [], []
    for part in parts:
        stats = jnp.dot(part[:, width:].astype(jnp.bfloat16), spread, preferred_element_type=jnp.float32)
        tops.append(stats[:, :width])
        totals.append(stats[:, width:])
    top = functools.reduce(jnp.maximum, tops)
    shares = [jnp.exp(t - top) * n for t, n in zip(tops, totals)]
    denom = functools.reduce(jnp.add, shares)
    numer = functools.reduce(jnp.add, [part[:, :width] * s for part, s in zip(parts, shares)])
    return (numer / (denom * SPAN)).astype(jnp.bfloat16)


def times(attended, weight):
    return lax.dot_general(attended, weight, (((1,), (1,)), ((), ())), preferred_element_type=jnp.float32)


def project_kernel(n_parts, w_ids, n_col, depth, where_ref, *refs):
    part_refs = refs[:n_parts]
    w_refs = refs[n_parts : n_parts + len(w_ids)]
    residual_ref, out_ref, whole_ref = refs[n_parts + len(w_ids) :]
    rows, features = out_ref.shape
    my_row, my_col = where_ref[0], where_ref[1]
    for ids, ref in zip(w_ids, w_refs):
        first = ref.shape[0] - len(ids) * depth
        for n, (a, b) in enumerate(ids):
            place = ((my_row ^ a) * n_col + (my_col ^ b)) * depth
            whole_ref[pl.ds(pl.multiple_of(place, 16), depth), :] = ref[first + n * depth : first + (n + 1) * depth, :]
    attended = merge([ref[:rows, :] for ref in part_refs])
    step = features // 4 if features % (4 * LANES) == 0 else features
    for at in range(0, features, step):
        here = slice(at, at + step)
        product = times(attended, whole_ref[here, :])
        out_ref[:, here] = (product + residual_ref[:, here].astype(jnp.float32)).astype(out_ref.dtype)


def call(kernel, shapes, where, arrays, scratch=()):
    smem = pl.BlockSpec(memory_space=pltpu.SMEM)
    vmem = pl.BlockSpec(memory_space=pltpu.VMEM)
    return pl.pallas_call(
        kernel,
        out_shape=shapes,
        in_specs=[smem] + [vmem] * len(arrays),
        out_specs=jax.tree.map(lambda _: vmem, shapes),
        scratch_shapes=list(scratch),
        compiler_params=pltpu.CompilerParams(vmem_limit_bytes=24 * 2**20),
    )(where, *arrays)


def local(queries, keys, values, block_mask, out_weight, residual):
    n_row, n_col = lax.axis_size("row"), lax.axis_size("col")
    top = n_col // 2
    near = range(1, max(top, 1))
    chips = range(2, n_row, 2)
    rows, depth = queries.shape[0], out_weight.shape[1]
    ride = depth % 16 == 0
    where = jnp.stack([lax.axis_index("row"), lax.axis_index("col")]).astype(jnp.int32)
    weight = out_weight.T

    pack = jnp.concatenate([keys, values, weight] if ride else [keys, values])
    gate = ()
    if top:
        far_k, far_v = swap(keys, "col", top), swap(values, "col", top)
        far_mask = swap(block_mask, "col", top)
        gate = (far_mask,)
    q_parts = {0: queries}
    for m in near:
        q_parts[m] = swap(queries, "col", m)
        gate += (q_parts[m],)
    kv_parts = {(0, 0): pack}
    for a in chips:
        kv_parts[a, 0] = swap(pack, "row", a)
    for a in (0, *chips):
        kv_parts[a | 1, 0] = swap(kv_parts[a, 0], "row", 1)
    masks = [where, block_mask.reshape(-1)]
    if top:
        kv_parts[0, top] = jnp.concatenate([after(far_k, *gate), far_v])
        for a in chips:
            kv_parts[a, top] = swap(kv_parts[0, top], "row", a)
        for a in (0, *chips):
            kv_parts[a | 1, top] = swap(kv_parts[a, top], "row", 1)
        masks.append(far_mask.reshape(-1))
    partial = attend(jnp.concatenate(masks), block_mask.shape, n_row, q_parts, kv_parts)

    parts = [partial]
    for n, m in enumerate(near, 1):
        sent = partial[n * rows : (n + 1) * rows].astype(jnp.float16)
        parts.append(swap(sent, "col", m).astype(jnp.float32))

    if ride:
        w_parts = [(kv_parts[a, 0], [(a, 0)]) for a in range(n_row)]
        ready = kv_parts[1, top]
        mine = [(weight, 0)]
        bit = top
        while bit:
            mine += [(swap(after(x, ready) if m else x, "col", bit), m | bit) for x, m in mine]
            bit //= 2
        for batch, gates in ((mine[1:-1], (ready,)), (mine[-1:], (ready, partial))):
            if not batch or not batch[0][1]:
                continue
            batch = [(after(x, *gates), m) for x, m in batch]
            block = jnp.concatenate([x for x, _ in batch]) if len(batch) > 1 else batch[0][0]
            held = {0: block}
            for a in chips:
                held[a] = swap(block, "row", a)
            for a in (0, *chips):
                held[a | 1] = swap(after(held[a], *parts[1:]), "row", 1)
            w_parts += [(x, [(a, m) for _, m in batch]) for a, x in held.items()]
    else:
        weight = lax.all_gather(weight, ("row", "col"), axis=0, tiled=True)
        w_parts, depth, n_col, where = [(weight, [(0, 0)])], weight.shape[0], 1, jnp.zeros_like(where)
    w_ids = [ids for _, ids in w_parts]
    arrays = [*parts, *(x for x, _ in w_parts), residual]
    scratch = [pltpu.VMEM((residual.shape[1], queries.shape[1]), jnp.bfloat16)]
    shape = jax.ShapeDtypeStruct(residual.shape, residual.dtype)
    return call(functools.partial(project_kernel, len(parts), w_ids, n_col, depth), shape, where, arrays, scratch)


def solution(mesh):
    placed = (
        P(("groups", "row", "col"), None),
        P(("groups", "col", "row"), None),
        P(("groups", "col", "row"), None),
        P(("groups", "row"), "col"),
        P(None, ("row", "col")),
        P(("groups", "row", "col"), None),
    )
    return jax.shard_map(
        local,
        mesh=mesh,
        in_specs=placed,
        out_specs=P(("groups", "row", "col"), None),
        check_vma=False,
    )
```

```python
import functools
import math

import jax
import jax.numpy as jnp
from jax import lax
from jax.experimental import pallas as pl
from jax.experimental.pallas import tpu as pltpu
from jax.sharding import PartitionSpec as P

HD = 128
BLK = 128
LANES = 128
PARTS = 3
SPAN = 8192.0


def swap(x, axis, mask):
    return lax.ppermute(x, axis, [(i, i ^ mask) for i in range(lax.axis_size(axis))])


def after(x, *others):
    return lax.optimization_barrier((x, *others))[0]


def split3(x):
    high = x.astype(jnp.bfloat16).astype(jnp.float32)
    rest = x - high
    middle = rest.astype(jnp.bfloat16).astype(jnp.float32)
    return (high, middle, rest - middle)


def attend_kernel(q_masks, k_masks, per_tile, mask_shape, place_ref, *refs):
    nq, nk = len(q_masks), len(k_masks)
    q_refs, kv_refs, out_ref = refs[:nq], refs[nq : nq + nk], refs[-1]
    rows, width = q_refs[0].shape
    heads = width // HD
    scale = 1.0 / math.sqrt(HD)
    my_row, my_col = place_ref[0], place_ref[1]
    keys = nk * rows
    piece_of_lane = lax.broadcasted_iota(jnp.int32, (1, keys), 1) // rows
    group = min(nq, 4)
    lane = lax.broadcasted_iota(jnp.int32, (group * rows, LANES), 1)
    for first in range(0, nq, group):
        chosen = range(first, first + group)
        lines = []
        for i in chosen:
            q_block = ((my_col ^ q_masks[i]) * rows) // BLK
            line = jnp.zeros((1, keys), jnp.float32)
            for j, (a, b) in enumerate(k_masks):
                k_block = ((my_row ^ a) * rows) // BLK
                at = 2 + q_block * mask_shape[1] + k_block
                if b:
                    at += mask_shape[0] * mask_shape[1]
                hidden = jnp.where(place_ref[at] == 1, 0.0, -jnp.inf)
                line = jnp.where(piece_of_lane == j, hidden, line)
            lines.append(jnp.broadcast_to(line, (rows, keys)))
        bias = jnp.concatenate(lines, axis=0)
        stats = jnp.zeros((group * rows, LANES), jnp.float32)
        here = slice(first * rows, (first + group) * rows)
        for h in range(heads):
            columns = slice(h * HD, (h + 1) * HD)
            q = jnp.concatenate([q_refs[i][:rows, columns] for i in chosen], axis=0)
            tops, totals, sums = [], [], []
            for tile in range(0, nk, per_tile):
                refs_here = kv_refs[tile : tile + per_tile]
                k = jnp.concatenate([r[:rows, columns] for r in refs_here], axis=0)
                v = jnp.concatenate([r[rows : 2 * rows, columns] for r in refs_here], axis=0)
                scores = lax.dot_general(
                    q, k, (((1,), (1,)), ((), ())), preferred_element_type=jnp.float32
                )
                scores = scores * scale + bias[:, tile * rows : (tile + per_tile) * rows]
                tops.append(jnp.max(scores, axis=1, keepdims=True))
                weights = jnp.exp(scores - tops[-1])
                totals.append(jnp.sum(weights, axis=1, keepdims=True))
                sums.append(jnp.dot(weights.astype(jnp.bfloat16), v, preferred_element_type=jnp.float32))
            top_score = functools.reduce(jnp.maximum, tops)
            factors = [jnp.exp(t - top_score) for t in tops]
            total = functools.reduce(jnp.add, [f * t for f, t in zip(factors, totals)])
            summed = functools.reduce(jnp.add, [f * t for f, t in zip(factors, sums)])
            out_ref[here, columns] = summed * (SPAN / total)
            for n, piece in enumerate(split3(top_score) + split3(total)):
                stats = jnp.where(lane == h * 2 * PARTS + n, piece, stats)
        out_ref[here, width:] = stats


def attend(place, mask_shape, per_tile, q_parts, kv_parts):
    q_masks, k_masks = tuple(q_parts), tuple(kv_parts)
    rows, width = q_parts[0].shape
    smem = pl.BlockSpec(memory_space=pltpu.SMEM)
    vmem = pl.BlockSpec(memory_space=pltpu.VMEM)
    arrays = [*q_parts.values(), *kv_parts.values()]
    return pl.pallas_call(
        functools.partial(attend_kernel, q_masks, k_masks, per_tile, mask_shape),
        out_shape=jax.ShapeDtypeStruct((len(q_masks) * rows, width + LANES), jnp.float32),
        in_specs=[smem] + [vmem] * len(arrays),
        out_specs=vmem,
        compiler_params=pltpu.CompilerParams(vmem_limit_bytes=24 * 2**20),
    )(place, *arrays)


def merge(parts):
    width = parts[0].shape[1] - LANES
    source = lax.broadcasted_iota(jnp.int32, (LANES, 2 * width), 0) // PARTS
    target = lax.broadcasted_iota(jnp.int32, (LANES, 2 * width), 1)
    target = target % width // HD * 2 + target // width
    spread = (source == target).astype(jnp.bfloat16)
    tops, totals = [], []
    for part in parts:
        stats = jnp.dot(part[:, width:].astype(jnp.bfloat16), spread, preferred_element_type=jnp.float32)
        tops.append(stats[:, :width])
        totals.append(stats[:, width:])
    top = functools.reduce(jnp.maximum, tops)
    shares = [jnp.exp(t - top) * n for t, n in zip(tops, totals)]
    denom = functools.reduce(jnp.add, shares)
    numer = functools.reduce(jnp.add, [part[:, :width] * s for part, s in zip(parts, shares)])
    return (numer / (denom * SPAN)).astype(jnp.bfloat16)


def times(attended, weight):
    return lax.dot_general(attended, weight, (((1,), (1,)), ((), ())), preferred_element_type=jnp.float32)


def place_weight(w_ids, n_col, depth, w_refs, whole_ref):
    my_row, my_col = (lax.axis_index("row"), lax.axis_index("col")) if len(w_ids) > 1 else (0, 0)
    for ids, ref in zip(w_ids, w_refs):
        first = ref.shape[0] - len(ids) * depth
        for n, (a, b) in enumerate(ids):
            place = ((my_row ^ a) * n_col + (my_col ^ b)) * depth
            whole_ref[pl.ds(pl.multiple_of(place, 16), depth), :] = ref[first + n * depth : first + (n + 1) * depth, :]


def merge_kernel(n_parts, w_ids, n_col, depth, *refs):
    part_refs, w_refs, (attended_ref, whole_ref) = refs[:n_parts], refs[n_parts:-2], refs[-2:]
    place_weight(w_ids, n_col, depth, w_refs, whole_ref)
    attended_ref[...] = merge([ref[: attended_ref.shape[0], :] for ref in part_refs])


def project_kernel(w_ids, n_col, depth, begun_ref, attended_ref, *refs):
    w_refs, (residual_ref, out_ref, whole_ref) = refs[: len(w_ids)], refs[len(w_ids) :]
    place_weight(w_ids, n_col, depth, w_refs, whole_ref)
    features = out_ref.shape[1]
    attended = attended_ref[...]
    step = features // 4 if features % (4 * LANES) == 0 else features
    for at in range(0, features, step):
        here = slice(at, at + step)
        product = times(attended, whole_ref[here, :])
        out_ref[:, here] = (product + residual_ref[:, here].astype(jnp.float32)).astype(out_ref.dtype)


def call(kernel, shapes, arrays, aliases=None):
    vmem = pl.BlockSpec(memory_space=pltpu.VMEM)
    return pl.pallas_call(
        kernel,
        out_shape=shapes,
        in_specs=[vmem] * len(arrays),
        out_specs=jax.tree.map(lambda _: vmem, shapes),
        input_output_aliases=aliases or {},
        compiler_params=pltpu.CompilerParams(vmem_limit_bytes=24 * 2**20),
    )(*arrays)


def local(queries, keys, values, block_mask, out_weight, residual):
    n_row, n_col = lax.axis_size("row"), lax.axis_size("col")
    top = n_col // 2
    near = range(1, max(top, 1))
    chips = range(2, n_row, 2)
    rows, depth = queries.shape[0], out_weight.shape[1]
    ride = depth % 16 == 0
    where = jnp.stack([lax.axis_index("row"), lax.axis_index("col")]).astype(jnp.int32)
    weight = out_weight.T

    pack = jnp.concatenate([keys, values, weight] if ride else [keys, values])
    gate = ()
    if top:
        far_k, far_v = swap(keys, "col", top), swap(values, "col", top)
        far_mask = swap(block_mask, "col", top)
        gate = (far_mask,)
    q_parts = {0: queries}
    for m in near:
        q_parts[m] = swap(queries, "col", m)
        gate += (q_parts[m],)
    kv_parts = {(0, 0): pack}
    for a in chips:
        kv_parts[a, 0] = swap(pack, "row", a)
    for a in (0, *chips):
        kv_parts[a | 1, 0] = swap(kv_parts[a, 0], "row", 1)
    masks = [where, block_mask.reshape(-1)]
    if top:
        kv_parts[0, top] = jnp.concatenate([after(far_k, *gate), far_v])
        for a in chips:
            kv_parts[a, top] = swap(kv_parts[0, top], "row", a)
        for a in (0, *chips):
            kv_parts[a | 1, top] = swap(kv_parts[a, top], "row", 1)
        masks.append(far_mask.reshape(-1))
    partial = attend(jnp.concatenate(masks), block_mask.shape, n_row, q_parts, kv_parts)

    parts = [partial]
    for n, m in enumerate(near, 1):
        sent = partial[n * rows : (n + 1) * rows].astype(jnp.float16)
        parts.append(swap(sent, "col", m).astype(jnp.float32))

    if ride:
        w_parts = [(kv_parts[a, 0], [(a, 0)]) for a in range(n_row)]
        ready = kv_parts[1, top]
        mine = [(weight, 0)]
        bit = top
        while bit:
            mine += [(swap(after(x, ready) if m else x, "col", bit), m | bit) for x, m in mine]
            bit //= 2
        for batch, gates in ((mine[1:-1], (ready,)), (mine[-1:], (ready, partial))):
            if not batch or not batch[0][1]:
                continue
            batch = [(after(x, *gates), m) for x, m in batch]
            block = jnp.concatenate([x for x, _ in batch]) if len(batch) > 1 else batch[0][0]
            held = {0: block}
            for a in chips:
                held[a] = swap(block, "row", a)
            for a in (0, *chips):
                held[a | 1] = swap(after(held[a], *parts[1:]), "row", 1)
            w_parts += [(x, [(a, m) for _, m in batch]) for a, x in held.items()]
    else:
        weight = lax.all_gather(weight, ("row", "col"), axis=0, tiled=True)
        w_parts, depth, n_col = [(weight, [(0, 0)])], weight.shape[0], 1
    soon = [w for w in w_parts if not w[1][0][0] & 1 or w[1][0][1] == 0]
    last = [w for w in w_parts if all(w is not other for other in soon)]
    whole = jax.ShapeDtypeStruct((residual.shape[1], queries.shape[1]), jnp.bfloat16)
    attended, begun = call(
        functools.partial(merge_kernel, len(parts), [ids for _, ids in soon], n_col, depth),
        [jax.ShapeDtypeStruct(queries.shape, queries.dtype), whole], [*parts, *(x for x, _ in soon)],
    )
    return call(
        functools.partial(project_kernel, [ids for _, ids in last], n_col, depth),
        [jax.ShapeDtypeStruct(residual.shape, residual.dtype), whole],
        [begun, attended, *(x for x, _ in last), residual], {0: 1},
    )[0]


def solution(mesh):
    placed = (
        P(("groups", "row", "col"), None),
        P(("groups", "col", "row"), None),
        P(("groups", "col", "row"), None),
        P(("groups", "row"), "col"),
        P(None, ("row", "col")),
        P(("groups", "row", "col"), None),
    )
    return jax.shard_map(
        local,
        mesh=mesh,
        in_specs=placed,
        out_specs=P(("groups", "row", "col"), None),
        check_vma=False,
    )
```

```python
import functools
import math

import jax
import jax.numpy as jnp
from jax import lax
from jax.experimental import pallas as pl
from jax.experimental.pallas import tpu as pltpu
from jax.sharding import PartitionSpec as P

HD = 128
BLK = 128
LANES = 128
PARTS = 3
SPAN = 8192.0


def swap(x, axis, mask):
    return lax.ppermute(x, axis, [(i, i ^ mask) for i in range(lax.axis_size(axis))])


def after(x, *others):
    return lax.optimization_barrier((x, *others))[0]


def split3(x):
    high = x.astype(jnp.bfloat16).astype(jnp.float32)
    rest = x - high
    middle = rest.astype(jnp.bfloat16).astype(jnp.float32)
    return (high, middle, rest - middle)


def attend_kernel(q_masks, k_masks, per_tile, seen_ref, *refs):
    nq, nk = len(q_masks), len(k_masks)
    q_refs, kv_refs, out_ref = refs[:nq], refs[nq : nq + nk], refs[-1]
    rows, width = q_refs[0].shape
    heads = width // HD
    scale = 1.0 / math.sqrt(HD)
    my_row, my_col = lax.axis_index("row"), lax.axis_index("col")
    visible = seen_ref[...]
    far_rows = seen_ref.shape[0] // 2
    q_line = lax.broadcasted_iota(jnp.int32, seen_ref.shape, 0)
    k_line = lax.broadcasted_iota(jnp.int32, seen_ref.shape, 1)
    keys = nk * rows
    piece_of_lane = lax.broadcasted_iota(jnp.int32, (1, keys), 1) // rows
    group = min(nq, 4)
    lane = lax.broadcasted_iota(jnp.int32, (group * rows, LANES), 1)
    for first in range(0, nq, group):
        chosen = range(first, first + group)
        lines = []
        for i in chosen:
            q_block = ((my_col ^ q_masks[i]) * rows) // BLK
            line = jnp.zeros((1, keys), jnp.float32)
            for j, (a, b) in enumerate(k_masks):
                k_block = ((my_row ^ a) * rows) // BLK
                here = (q_line == q_block + (far_rows if b else 0)) & (k_line == k_block)
                seen = jnp.sum(jnp.where(here, visible, 0.0), axis=(0, 1), keepdims=True)
                hidden = jnp.where(seen > 0.5, 0.0, -jnp.inf)
                line = jnp.where(piece_of_lane == j, hidden, line)
            lines.append(jnp.broadcast_to(line, (rows, keys)))
        bias = jnp.concatenate(lines, axis=0)
        stats = jnp.zeros((group * rows, LANES), jnp.float32)
        here = slice(first * rows, (first + group) * rows)
        for h in range(heads):
            columns = slice(h * HD, (h + 1) * HD)
            q = jnp.concatenate([q_refs[i][:rows, columns] for i in chosen], axis=0)
            tops, totals, sums = [], [], []
            for tile in range(0, nk, per_tile):
                refs_here = kv_refs[tile : tile + per_tile]
                k = jnp.concatenate([r[:rows, columns] for r in refs_here], axis=0)
                v = jnp.concatenate([r[rows : 2 * rows, columns] for r in refs_here], axis=0)
                scores = lax.dot_general(
                    q, k, (((1,), (1,)), ((), ())), preferred_element_type=jnp.float32
                )
                scores = scores * scale + bias[:, tile * rows : (tile + per_tile) * rows]
                tops.append(jnp.max(scores, axis=1, keepdims=True))
                weights = jnp.exp(scores - tops[-1])
                totals.append(jnp.sum(weights, axis=1, keepdims=True))
                sums.append(jnp.dot(weights.astype(jnp.bfloat16), v, preferred_element_type=jnp.float32))
            top_score = functools.reduce(jnp.maximum, tops)
            factors = [jnp.exp(t - top_score) for t in tops]
            total = functools.reduce(jnp.add, [f * t for f, t in zip(factors, totals)])
            summed = functools.reduce(jnp.add, [f * t for f, t in zip(factors, sums)])
            out_ref[here, columns] = summed * (SPAN / total)
            for n, piece in enumerate(split3(top_score) + split3(total)):
                stats = jnp.where(lane == h * 2 * PARTS + n, piece, stats)
        out_ref[here, width:] = stats


def attend(masks, per_tile, q_parts, kv_parts):
    q_masks, k_masks = tuple(q_parts), tuple(kv_parts)
    rows, width = q_parts[0].shape
    vmem = pl.BlockSpec(memory_space=pltpu.VMEM)
    arrays = [*q_parts.values(), *kv_parts.values()]
    return pl.pallas_call(
        functools.partial(attend_kernel, q_masks, k_masks, per_tile),
        out_shape=jax.ShapeDtypeStruct((len(q_masks) * rows, width + LANES), jnp.float32),
        in_specs=[vmem] * (1 + len(arrays)),
        out_specs=vmem,
        compiler_params=pltpu.CompilerParams(vmem_limit_bytes=24 * 2**20),
    )(masks, *arrays)


def merge(parts):
    width = parts[0].shape[1] - LANES
    source = lax.broadcasted_iota(jnp.int32, (LANES, 2 * width), 0) // PARTS
    target = lax.broadcasted_iota(jnp.int32, (LANES, 2 * width), 1)
    target = target % width // HD * 2 + target // width
    spread = (source == target).astype(jnp.bfloat16)
    tops, totals = [], []
    for part in parts:
        stats = jnp.dot(part[:, width:].astype(jnp.bfloat16), spread, preferred_element_type=jnp.float32)
        tops.append(stats[:, :width])
        totals.append(stats[:, width:])
    top = functools.reduce(jnp.maximum, tops)
    shares = [jnp.exp(t - top) * n for t, n in zip(tops, totals)]
    denom = functools.reduce(jnp.add, shares)
    numer = functools.reduce(jnp.add, [part[:, :width] * s for part, s in zip(parts, shares)])
    return (numer / (denom * SPAN)).astype(jnp.bfloat16)


def times(attended, weight):
    return lax.dot_general(attended, weight, (((1,), (1,)), ((), ())), preferred_element_type=jnp.float32)


def place_weight(w_ids, n_col, depth, w_refs, whole_ref):
    my_row, my_col = (lax.axis_index("row"), lax.axis_index("col")) if len(w_ids) > 1 else (0, 0)
    for ids, ref in zip(w_ids, w_refs):
        first = ref.shape[0] - len(ids) * depth
        for n, (a, b) in enumerate(ids):
            place = ((my_row ^ a) * n_col + (my_col ^ b)) * depth
            whole_ref[pl.ds(pl.multiple_of(place, 16), depth), :] = ref[first + n * depth : first + (n + 1) * depth, :]


def merge_kernel(n_parts, w_ids, n_col, depth, *refs):
    part_refs, w_refs, (attended_ref, whole_ref) = refs[:n_parts], refs[n_parts:-2], refs[-2:]
    place_weight(w_ids, n_col, depth, w_refs, whole_ref)
    attended_ref[...] = merge([ref[: attended_ref.shape[0], :] for ref in part_refs])


def project_kernel(w_ids, n_col, depth, begun_ref, attended_ref, *refs):
    w_refs, (residual_ref, out_ref, whole_ref) = refs[: len(w_ids)], refs[len(w_ids) :]
    place_weight(w_ids, n_col, depth, w_refs, whole_ref)
    features = out_ref.shape[1]
    attended = attended_ref[...]
    step = features // 4 if features % (4 * LANES) == 0 else features
    for at in range(0, features, step):
        here = slice(at, at + step)
        product = times(attended, whole_ref[here, :])
        out_ref[:, here] = (product + residual_ref[:, here].astype(jnp.float32)).astype(out_ref.dtype)


def call(kernel, shapes, arrays, aliases=None):
    vmem = pl.BlockSpec(memory_space=pltpu.VMEM)
    return pl.pallas_call(
        kernel,
        out_shape=shapes,
        in_specs=[vmem] * len(arrays),
        out_specs=jax.tree.map(lambda _: vmem, shapes),
        input_output_aliases=aliases or {},
        compiler_params=pltpu.CompilerParams(vmem_limit_bytes=24 * 2**20),
    )(*arrays)


def local(queries, keys, values, block_mask, out_weight, residual):
    n_row, n_col = lax.axis_size("row"), lax.axis_size("col")
    top = n_col // 2
    near = range(1, max(top, 1))
    chips = range(2, n_row, 2)
    rows, depth = queries.shape[0], out_weight.shape[1]
    ride = depth % 16 == 0
    weight = out_weight.T

    pack = jnp.concatenate([keys, values, weight] if ride else [keys, values])
    gate = ()
    if top:
        far_k, far_v = swap(keys, "col", top), swap(values, "col", top)
        far_mask = swap(block_mask, "col", top)
        gate = (far_mask,)
    q_parts = {0: queries}
    for m in near:
        q_parts[m] = swap(queries, "col", m)
        gate += (q_parts[m],)
    kv_parts = {(0, 0): pack}
    for a in chips:
        kv_parts[a, 0] = swap(pack, "row", a)
    for a in (0, *chips):
        kv_parts[a | 1, 0] = swap(kv_parts[a, 0], "row", 1)
    masks = jnp.concatenate([block_mask, far_mask if top else block_mask]).astype(jnp.float32)
    if top:
        kv_parts[0, top] = jnp.concatenate([after(far_k, *gate), far_v])
        for a in chips:
            kv_parts[a, top] = swap(kv_parts[0, top], "row", a)
        for a in (0, *chips):
            kv_parts[a | 1, top] = swap(kv_parts[a, top], "row", 1)
    partial = attend(masks, n_row, q_parts, kv_parts)

    parts = [partial]
    for n, m in enumerate(near, 1):
        sent = partial[n * rows : (n + 1) * rows].astype(jnp.float16)
        parts.append(swap(sent, "col", m).astype(jnp.float32))

    if ride:
        w_parts = [(kv_parts[a, 0], [(a, 0)]) for a in range(n_row)]
        ready = kv_parts[1, top]
        mine = [(weight, 0)]
        bit = top
        while bit:
            mine += [(swap(after(x, ready) if m else x, "col", bit), m | bit) for x, m in mine]
            bit //= 2
        for batch, gates in ((mine[1:-1], (ready,)), (mine[-1:], (ready, partial))):
            if not batch or not batch[0][1]:
                continue
            batch = [(after(x, *gates), m) for x, m in batch]
            block = jnp.concatenate([x for x, _ in batch]) if len(batch) > 1 else batch[0][0]
            held = {0: block}
            for a in chips:
                held[a] = swap(block, "row", a)
            for a in (0, *chips):
                held[a | 1] = swap(after(held[a], *parts[1:]), "row", 1)
            w_parts += [(x, [(a, m) for _, m in batch]) for a, x in held.items()]
    else:
        weight = lax.all_gather(weight, ("row", "col"), axis=0, tiled=True)
        w_parts, depth, n_col = [(weight, [(0, 0)])], weight.shape[0], 1
    soon = [w for w in w_parts if not w[1][0][0] & 1 or w[1][0][1] == 0]
    last = [w for w in w_parts if all(w is not other for other in soon)]
    whole = jax.ShapeDtypeStruct((residual.shape[1], queries.shape[1]), jnp.bfloat16)
    attended, begun = call(
        functools.partial(merge_kernel, len(parts), [ids for _, ids in soon], n_col, depth),
        [jax.ShapeDtypeStruct(queries.shape, queries.dtype), whole], [*parts, *(x for x, _ in soon)],
    )
    return call(
        functools.partial(project_kernel, [ids for _, ids in last], n_col, depth),
        [jax.ShapeDtypeStruct(residual.shape, residual.dtype), whole],
        [begun, attended, *(x for x, _ in last), residual], {0: 1},
    )[0]


def solution(mesh):
    placed = (
        P(("groups", "row", "col"), None),
        P(("groups", "col", "row"), None),
        P(("groups", "col", "row"), None),
        P(("groups", "row"), "col"),
        P(None, ("row", "col")),
        P(("groups", "row", "col"), None),
    )
    return jax.shard_map(
        local,
        mesh=mesh,
        in_specs=placed,
        out_specs=P(("groups", "row", "col"), None),
        check_vma=False,
    )
```
